768 devices in a mesh: blk: 24 (over z_hi, x, core), grp: 32 (over y, z_lo).
Axes of the slice: x: 4, y: 8, z: 12 (z_hi: 3, z_lo: 4; z = z_hi * 4 + z_lo), core: 2. Of those that a mesh axis runs over, the one named last changes fastest.
Arguments:
- picture_vectors: bfloat16 [196608, 1152], P(('blk', 'grp')), may hold values from -0.1875 to 0.1875
- sentence_vectors: bfloat16 [196608, 1152], P(('blk', 'grp')), may hold values from -0.1875 to 0.1875
- sharpness_factor: float32 [1], replicated, may hold values from 20 to 60
- additive_shift_term: float32 [1], replicated, may hold values from -3 to 0
- upstream_adjoint: float32 [1], replicated, may hold values from 256 to 1024
Outputs:
- grad_images: bfloat16 [196608, 1152], P(('blk', 'grp'))
- grad_texts: bfloat16 [196608, 1152], P(('blk', 'grp'))
The draws below stay inside these ranges and needn't reach their ends.
All inputs are finite; a program needn't handle non-finite values.
Results may differ from the reference program's by a relative error of at most 0.0056.
Values may be sent and summed in bfloat16 or wider, within the bound.
A program may use at most 32 MiB of HBM per device.

```python
import math
import jax
import jax.numpy as jnp

D = 1152
ROWS = 256
STEPS = 3
PAIR_COUNT = 196608
N_BLK = 24
N_GRP = 32


def level_of(rng, shape, shards, least, top_value):
    gain = 1.0
    for dim, shards_of in shards:
        heights = jax.random.uniform(jax.random.fold_in(jax.random.fold_in(rng, 6), dim), (shards_of,), jnp.float32, least / len(shards), top_value / len(shards))
        gain = gain * jnp.repeat(jnp.exp(heights), shape[dim] // shards_of).reshape((-1,) + (1,) * (len(shape) - 1 - dim))
    return gain


def bell_draw(rng, shape, scale, bound, cuts=(), held_as=jnp.bfloat16):
    array = jax.random.normal(rng, shape, jnp.float32) * scale
    if len(cuts) > 0:
        array = level_of(rng, shape, cuts, -0.22, 0.18) * array
    return jnp.clip(array, min=-bound, max=bound).astype(held_as)


def setup_inputs(seed: int = 0) -> dict:
    streams_of = jax.random.split(jax.random.key(seed), 6)
    picture_vectors = bell_draw(streams_of[0], (PAIR_COUNT, D), D ** -0.5, 0.1875, ((0, 768),))
    sentence_vectors = bell_draw(streams_of[1], (PAIR_COUNT, D), D ** -0.5, 0.1875, ((0, 768),))
    sharpness_factor = jnp.clip(jnp.exp(jax.random.uniform(streams_of[2], (1,), jnp.float32, math.log(20.0), math.log(60.0))), 20.0, 60.0)
    additive_shift_term = jnp.clip(jax.random.uniform(streams_of[3], (1,), jnp.float32, -3.0, 0.0), -3.0, 0.0)
    upstream_adjoint = jnp.clip(jnp.exp(jax.random.uniform(streams_of[4], (1,), jnp.float32, math.log(256.0), math.log(1024.0))), 256.0, 1024.0)
    return dict(picture_vectors=picture_vectors, sentence_vectors=sentence_vectors, sharpness_factor=sharpness_factor, additive_shift_term=additive_shift_term, upstream_adjoint=upstream_adjoint)


def reference(picture_vectors, sentence_vectors, sharpness_factor, additive_shift_term, upstream_adjoint):
    img_blocks = picture_vectors.reshape(N_BLK, N_GRP, ROWS, D)
    txt_blocks = sentence_vectors.reshape(N_BLK, N_GRP, ROWS, D)
    exp_sharpness = sharpness_factor[0]
    shifted_affinity = additive_shift_term[0]
    multiplier_matrix = upstream_adjoint[0] * exp_sharpness / PAIR_COUNT
    eye = (jnp.arange(ROWS)[:, None] == jnp.arange(ROWS)[None, :]).astype(jnp.float32)
    grad_img = jnp.zeros((N_BLK, N_GRP, ROWS, D), jnp.float32)
    totals = []
    for reach in range(2):
        parts = []
        for step in range(STEPS):
            met = jnp.roll(txt_blocks, (step, reach), axis=(0, 1)).astype(jnp.float32)
            similarity_matrix = jnp.einsum("bgid,bgjd->bgij", img_blocks.astype(jnp.float32), met)
            likelihood_matrix = jax.nn.sigmoid(exp_sharpness * similarity_matrix + shifted_affinity)
            if step == 0 and reach == 0:
                likelihood_matrix = likelihood_matrix - eye[None, None, :, :]
            weight_factors = (multiplier_matrix * likelihood_matrix).astype(jnp.bfloat16).astype(jnp.float32)
            grad_img = grad_img + jnp.einsum("bgij,bgjd->bgid", weight_factors, met)
            part = jnp.einsum("bgij,bgid->bgjd", weight_factors, img_blocks.astype(jnp.float32))
            parts.append(jnp.roll(part, (-step, -reach), axis=(0, 1)))
        carried = parts[STEPS - 1]
        for step in range(STEPS - 2, -1, -1):
            carried = carried.astype(jnp.bfloat16).astype(jnp.float32) + parts[step]
        totals.append(carried)
    caption_gradient = totals[0] + totals[1].astype(jnp.bfloat16).astype(jnp.float32)
    return (grad_img.reshape(PAIR_COUNT, D).astype(jnp.bfloat16), caption_gradient.reshape(PAIR_COUNT, D).astype(jnp.bfloat16))
```

```python
import functools

import jax
import jax.numpy as jnp
from jax import lax
from jax.experimental import pallas as pl
from jax.experimental.pallas import tpu as pltpu
from jax.sharding import PartitionSpec as P

MESH = pl.DeviceIdType.MESH
ROWS = 256
D = 1152
PIECE = 64
PAIRS = 196608
N_X, N_Y, N_HI, N_LO = 4, 8, 3, 4


def device(hi, x, core, y, lo):
    return ((hi * N_X + x) * 2 + core, y * N_LO + lo)


def kernel(
    sharp_ref,
    shift_ref,
    adj_ref,
    img_ref,
    txt_ref,
    gimg_ref,
    gtxt_ref,
    texts,
    images,
    weights,
    hop_img,
    hop_grad,
    sib_out,
    sib_in,
    next_out,
    next_in,
    text_out,
    text_in,
    load_sem,
    send_sem,
    recv_sem,
):
    blk = lax.axis_index("blk")
    grp = lax.axis_index("grp")
    core = lax.rem(blk, 2)
    x = lax.rem(lax.div(blk, 2), N_X)
    hi = lax.div(blk, 2 * N_X)
    grp_next = (blk, lax.rem(grp + 1, N_Y * N_LO))
    grp_prev = (blk, lax.rem(grp + N_Y * N_LO - 1, N_Y * N_LO))
    sibling = (blk + 1 - 2 * core, grp)
    hi_up = lax.rem(hi + 1, N_HI)
    hi_down = lax.rem(hi + N_HI - 1, N_HI)

    def line(which, at_hi):
        return ((at_hi * N_X + which) * 2 + core, grp)

    load_i = pltpu.make_async_copy(img_ref, images.at[pl.ds(0, ROWS)], load_sem.at[0])
    load_t = pltpu.make_async_copy(txt_ref, texts.at[pl.ds(0, ROWS)], load_sem.at[1])
    load_i.start()
    load_t.start()

    barrier = pltpu.get_barrier_semaphore()

    def greet(target):
        pl.semaphore_signal(barrier, inc=1, device_id=target, device_id_type=MESH)

    greet(grp_next)
    greet(grp_prev)
    greet(sibling)
    for step in range(1, N_X):
        greet(line(lax.rem(x + step, N_X), hi))

    @pl.when(x == N_X - 1)
    def _():
        for which in range(N_X):
            greet(line(which, hi_up))

    @pl.when(x == 0)
    def _():
        for which in range(N_X):
            greet(line(which, hi_down))

    sharp = sharp_ref[0]
    shift = shift_ref[0]
    scale = adj_ref[0] * sharp / PAIRS

    def make_weights(image, text):
        logits = lax.dot_general(
            images[pl.ds(image * ROWS, ROWS), :],
            texts[pl.ds(text * ROWS, ROWS), :],
            (((1,), (1,)), ((), ())),
            preferred_element_type=jnp.float32,
        )
        likely = jax.nn.sigmoid(sharp * logits + shift)
        if image == 0 and text == 0:
            cols = lax.broadcasted_iota(jnp.int32, likely.shape, 1)
            rows = lax.broadcasted_iota(jnp.int32, likely.shape, 0)
            likely = likely - (cols == rows).astype(jnp.float32)
        weights[pl.ds(image * ROWS, ROWS), pl.ds(text * ROWS, ROWS)] = (
            scale * likely
        ).astype(jnp.bfloat16)

    def image_grad(image):
        return jnp.dot(
            weights[pl.ds(image * ROWS, ROWS), :],
            texts[...],
            preferred_element_type=jnp.float32,
        )

    def text_grad(text):
        return lax.dot_general(
            weights[:, pl.ds(text * ROWS, ROWS)],
            images[...],
            (((0,), (0,)), ((), ())),
            preferred_element_type=jnp.float32,
        )

    def send(src, dst, which, arrival, target):
        return pltpu.make_async_remote_copy(
            src_ref=src,
            dst_ref=dst,
            send_sem=send_sem.at[which],
            recv_sem=recv_sem.at[arrival],
            device_id=target,
            device_id_type=MESH,
        )

    own_i = images.at[pl.ds(0, ROWS)]
    got_s = images.at[pl.ds(ROWS, ROWS)]
    got_x = images.at[pl.ds(2 * ROWS, ROWS)]

    def piece(ref, which, base=0):
        return ref.at[pl.ds(base + which * PIECE, PIECE)]

    load_i.wait()
    load_t.wait()
    make_weights(0, 0)
    pl.semaphore_wait(barrier, 8)

    send_text = send(texts.at[pl.ds(0, ROWS)], texts.at[pl.ds(ROWS, ROWS)], 0, 0, grp_next)
    send_text.start()
    send_image = send(own_i, got_x, 1, 1, line(lax.rem(x + N_X - 1, N_X), hi))
    send_first = send(
        piece(images, 0), piece(images, 0, 2 * ROWS), 1, 1, line(N_X - 1, hi_down)
    )
    to_relay = [
        send(piece(images, q), hop_img, 1 + q, 3, line(q, hi)) for q in range(1, N_X)
    ]
    relay_image = send(
        hop_img, piece(images, x, 2 * ROWS), 5, 1, line(N_X - 1, hi_down)
    )
    send_sib = send(own_i, got_s, 6, 2, sibling)
    forward_sib = send(got_x, got_s, 6, 2, sibling)

    @pl.when(x > 0)
    def _():
        send_image.start()

    @pl.when(x == 0)
    def _():
        for copy in to_relay:
            copy.start()
        send_first.start()

    @pl.when(core == 1)
    def _():
        send_sib.start()

    @pl.when(x > 0)
    def _():
        send(hop_img, hop_img, 1, 3, sibling).wait_recv()
        relay_image.start()

    wait_x = send(got_x, got_x, 1, 1, sibling)

    @pl.when(core == 0)
    def _():
        wait_x.wait_recv()
        forward_sib.start()

    send_text.wait_recv()
    make_weights(0, 1)

    send_sib.wait_recv()
    make_weights(1, 0)
    make_weights(1, 1)
    sib_out[...] = image_grad(1).astype(jnp.bfloat16)
    return_sib = send(sib_out, sib_in, 7, 4, sibling)
    return_sib.start()

    @pl.when(core == 1)
    def _():
        wait_x.wait_recv()

    make_weights(2, 0)
    make_weights(2, 1)
    grad_x = image_grad(2)

    @pl.when(core == 0)
    def _():
        return_sib.wait_recv()
        next_out[...] = (grad_x + sib_in[...].astype(jnp.float32)).astype(jnp.bfloat16)

    @pl.when(core == 1)
    def _():
        next_out[...] = grad_x.astype(jnp.bfloat16)

    send_grad = send(next_out, next_in, 8, 5, line(lax.rem(x + 1, N_X), hi))
    send_last = send(
        piece(next_out, N_X - 1), piece(next_in, N_X - 1), 8, 5, line(0, hi_up)
    )
    grad_to_relay = [
        send(piece(next_out, q), hop_grad, 9 + q, 7, line(q, hi)) for q in range(N_X - 1)
    ]
    relay_grad = send(hop_grad, piece(next_in, x), 12, 5, line(0, hi_up))

    @pl.when(x < N_X - 1)
    def _():
        send_grad.start()

    @pl.when(x == N_X - 1)
    def _():
        for copy in grad_to_relay:
            copy.start()
        send_last.start()

    text_out[...] = text_grad(1).astype(jnp.bfloat16)
    return_text = send(text_out, text_in, 13, 6, grp_prev)
    return_text.start()

    @pl.when(x < N_X - 1)
    def _():
        send(hop_grad, hop_grad, 12, 7, sibling).wait_recv()
        relay_grad.start()

    grad_t = text_grad(0)
    grad_i = image_grad(0)

    @pl.when(core == 1)
    def _():
        return_sib.wait_recv()

    send_grad.wait_recv()

    @pl.when(core == 0)
    def _():
        gimg_ref[...] = (grad_i + next_in[...].astype(jnp.float32)).astype(jnp.bfloat16)

    @pl.when(core == 1)
    def _():
        gimg_ref[...] = (
            grad_i
            + next_in[...].astype(jnp.float32)
            + sib_in[...].astype(jnp.float32)
        ).astype(jnp.bfloat16)

    return_text.wait_recv()
    gtxt_ref[...] = (grad_t + text_in[...].astype(jnp.float32)).astype(jnp.bfloat16)

    send_text.wait_send()

    @pl.when(x > 0)
    def _():
        send_image.wait_send()
        relay_image.wait_send()

    @pl.when(x == 0)
    def _():
        send_first.wait_send()
        for copy in to_relay:
            copy.wait_send()

    send_sib.wait_send()
    return_sib.wait_send()

    @pl.when(x < N_X - 1)
    def _():
        send_grad.wait_send()
        relay_grad.wait_send()

    @pl.when(x == N_X - 1)
    def _():
        send_last.wait_send()
        for copy in grad_to_relay:
            copy.wait_send()

    return_text.wait_send()


def on_device(img, txt, sharp, shift, adj):
    shard = jax.ShapeDtypeStruct((ROWS, D), jnp.bfloat16)

    def half(rows, cols=D):
        return pltpu.VMEM((rows, cols), jnp.bfloat16)

    return pl.pallas_call(
        kernel,
        out_shape=(shard, shard),
        in_specs=[pl.BlockSpec(memory_space=pltpu.SMEM)] * 3
        + [pl.BlockSpec(memory_space=pl.ANY)] * 2,
        out_specs=[pl.BlockSpec(memory_space=pltpu.VMEM)] * 2,
        scratch_shapes=[
            half(2 * ROWS),
            half(3 * ROWS),
            half(3 * ROWS, 2 * ROWS),
            half(PIECE),
            half(PIECE),
            half(ROWS),
            half(ROWS),
            half(ROWS),
            half(ROWS),
            half(ROWS),
            half(ROWS),
            pltpu.SemaphoreType.DMA((2,)),
            pltpu.SemaphoreType.DMA((14,)),
            pltpu.SemaphoreType.DMA((8,)),
        ],
        compiler_params=pltpu.CompilerParams(
            collective_id=0, has_side_effects=True, vmem_limit_bytes=48 << 20
        ),
        cost_estimate=pl.CostEstimate(
            flops=18 * 2 * ROWS * ROWS * D, bytes_accessed=4 * ROWS * D * 2, transcendentals=6 * ROWS * ROWS
        ),
    )(sharp, shift, adj, img, txt)


def solution(mesh):
    return jax.shard_map(
        on_device,
        mesh=mesh,
        in_specs=(P(("blk", "grp"), None), P(("blk", "grp"), None), P(), P(), P()),
        out_specs=(P(("blk", "grp"), None), P(("blk", "grp"), None)),
        check_vma=False,
    )
```

```python
import functools

import jax
import jax.numpy as jnp
from jax import lax
from jax.experimental import pallas as pl
from jax.experimental.pallas import tpu as pltpu
from jax.sharding import PartitionSpec as P

MESH = pl.DeviceIdType.MESH
ROWS = 256
D = 1152
HALF = 128
PIECE = 32
PAIRS = 196608
N_X, N_Y, N_HI, N_LO = 4, 8, 3, 4


def device(hi, x, core, y, lo):
    return ((hi * N_X + x) * 2 + core, y * N_LO + lo)


def kernel(
    sharp_ref,
    shift_ref,
    adj_ref,
    img_ref,
    txt_ref,
    gimg_ref,
    gtxt_ref,
    texts,
    images,
    weights,
    hop_img,
    hop_grad,
    next_out,
    next_in,
    part_out,
    part_in,
    text_out,
    text_in,
    load_sem,
    send_sem,
    recv_sem,
    far_sem,
):
    blk = lax.axis_index("blk")
    grp = lax.axis_index("grp")
    core = lax.rem(blk, 2)
    x = lax.rem(lax.div(blk, 2), N_X)
    hi = lax.div(blk, 2 * N_X)
    grp_lo = lax.rem(grp, N_LO)
    grp_next = (blk, lax.rem(grp + 1, N_Y * N_LO))
    grp_prev = (blk, lax.rem(grp + N_Y * N_LO - 1, N_Y * N_LO))
    sibling = (blk + 1 - 2 * core, grp)
    hi_up = lax.rem(hi + 1, N_HI)
    hi_down = lax.rem(hi + N_HI - 1, N_HI)

    def line(which, at_hi):
        return ((at_hi * N_X + which) * 2 + core, grp)

    own_t, near_t, sib_t, sib_near_t = (
        texts.at[pl.ds(ROWS * n, ROWS)] for n in range(4)
    )
    own_i = images.at[pl.ds(0, ROWS)]

    load_i = pltpu.make_async_copy(img_ref, own_i, load_sem.at[0])
    load_t = pltpu.make_async_copy(txt_ref, own_t, load_sem.at[1])
    load_i.start()
    load_t.start()

    barrier = pltpu.get_barrier_semaphore()

    def greet(target):
        pl.semaphore_signal(barrier, inc=1, device_id=target, device_id_type=MESH)

    greet(grp_prev)
    greet(sibling)

    @pl.when(x == 0)
    def _():
        greet(line(1, hi))

    @pl.when(x > 0)
    def _():
        greet(line(0, hi))

    @pl.when(x == 1)
    def _():
        greet(line(2, hi))

    @pl.when(x < N_X - 1)
    def _():
        greet(line(N_X - 1, hi))

    wraps = hi == 0

    @pl.when((x == N_X - 1) & (hi < N_HI - 1))
    def _():
        for which in range(N_X):
            greet(line(which, hi_up))

    @pl.when(wraps)
    def _():
        greet(line(N_X - 1, hi_down))

    sharp = sharp_ref[0]
    shift = shift_ref[0]
    scale = adj_ref[0] * sharp / PAIRS

    def make_weights(row, rows, text, own_pair=False):
        logits = lax.dot_general(
            images[pl.ds(row, rows), :],
            texts[pl.ds(text * ROWS, ROWS), :],
            (((1,), (1,)), ((), ())),
            preferred_element_type=jnp.float32,
        )
        likely = jax.nn.sigmoid(sharp * logits + shift)
        if own_pair:
            cols = lax.broadcasted_iota(jnp.int32, likely.shape, 1)
            at_row = lax.broadcasted_iota(jnp.int32, likely.shape, 0)
            likely = likely - (cols == at_row).astype(jnp.float32)
        weights[pl.ds(row, rows), pl.ds(text * ROWS, ROWS)] = (scale * likely).astype(
            jnp.bfloat16
        )

    def image_grad(row, rows, n_texts):
        return jnp.dot(
            weights[pl.ds(row, rows), pl.ds(0, n_texts * ROWS)],
            texts[pl.ds(0, n_texts * ROWS), :],
            preferred_element_type=jnp.float32,
        )

    def text_grad(row, rows, text):
        return lax.dot_general(
            weights[pl.ds(row, rows), pl.ds(text * ROWS, ROWS)],
            images[pl.ds(row, rows), :],
            (((0,), (0,)), ((), ())),
            preferred_element_type=jnp.float32,
        )

    def send(src, dst, which, arrival, target):
        return pltpu.make_async_remote_copy(
            src_ref=src,
            dst_ref=dst,
            send_sem=send_sem.at[which],
            recv_sem=recv_sem.at[arrival],
            device_id=target,
            device_id_type=MESH,
        )

    def arrived(ref, arrival):
        send(ref, ref, 0, arrival, sibling).wait_recv()

    def half(ref, h, base=0):
        return ref.at[pl.ds(base + h * HALF, HALF)]

    def piece(ref, h, q, base=0):
        return ref.at[pl.ds(base + h * HALF + q * PIECE, PIECE)]

    up_line = line(0, hi_up)
    down_line = line(N_X - 1, hi_down)
    x_up = line(lax.rem(x + 1, N_X), hi)
    x_down = line(lax.rem(x + N_X - 1, N_X), hi)

    send_text = send(own_t, near_t, 0, 0, grp_next)
    share_text = send(own_t, sib_t, 1, 1, sibling)
    share_near = send(near_t, sib_near_t, 2, 2, sibling)
    image_direct, image_first, image_spread, image_relay = [], [], [], []
    grad_direct, grad_last, grad_spread, grad_relay = [], [], [], []
    for h in range(2):
        image_direct.append(
            send(half(images, h), half(images, h, ROWS), 3 + h, 3 + h, x_down)
        )
        image_first.append(
            send(piece(images, h, 0), piece(images, h, 0, ROWS), 3 + h, 3 + h, down_line)
        )
        image_spread.append(
            [
                send(piece(images, h, q), hop_img.at[h], 5 + 3 * h + q, 5 + h, line(q, hi))
                for q in range(1, N_X)
            ]
        )
        image_relay.append(
            send(hop_img.at[h], piece(images, h, x, ROWS), 12 + h, 3 + h, down_line)
        )
        grad_direct.append(send(half(next_out, h), half(next_in, h), 14 + h, 7 + h, x_up))
        grad_last.append(
            send(
                piece(next_out, h, N_X - 1),
                piece(next_in, h, N_X - 1),
                14 + h,
                7 + h,
                up_line,
            )
        )
        grad_spread.append(
            [
                send(piece(next_out, h, q), hop_grad.at[h], 16 + 3 * h + q, 9 + h, line(q, hi))
                for q in range(N_X - 1)
            ]
        )
        grad_relay.append(
            send(hop_grad.at[h], piece(next_in, h, x), 22 + h, 7 + h, up_line)
        )
    share_part = [send(part_out.at[t], part_in.at[t], 24 + t, 11 + t, sibling) for t in range(2)]
    return_text = send(text_out, text_in, 26, 13, grp_prev)

    load_i.wait()
    load_t.wait()
    make_weights(0, ROWS, 0, own_pair=True)
    first = jnp.where((x == 0) | (x == N_X - 1), 5, 3)
    first = first + jnp.where(hi > 0, 1, 0)
    first = first + jnp.where((x == N_X - 1) & (hi == N_HI - 1), N_X, 0)
    pl.semaphore_wait(barrier, first)

    @pl.when((x == N_X - 1) & (hi == N_HI - 1))
    def _():
        for which in range(N_X):
            pl.semaphore_signal(
                far_sem, inc=1, device_id=line(which, hi_up), device_id_type=MESH
            )

    def await_far():
        @pl.when(wraps)
        def _():
            pl.semaphore_wait(far_sem, 1)

    @pl.when(x == 0)
    def _():
        for h in range(2):
            for copy in image_spread[h]:
                copy.start()

    @pl.when(x > 0)
    def _():
        for h in range(2):
            image_direct[h].start()

    send_text.start()
    share_text.start()

    await_far()

    @pl.when(x == 0)
    def _():
        for h in (0,):
            image_first[h].start()

    @pl.when(x > 0)
    def _():
        for h in (0,):
            arrived(hop_img.at[h], 5 + h)
            image_relay[h].start()

    share_text.wait_recv()

    @pl.when(core == 1)
    def _():
        make_weights(0, ROWS, 2)

    send_text.wait_recv()
    share_near.start()
    @pl.when(x == 0)
    def _():
        for h in (1,):
            image_first[h].start()

    @pl.when(x > 0)
    def _():
        for h in (1,):
            arrived(hop_img.at[h], 5 + h)
            image_relay[h].start()


    make_weights(0, ROWS, 1)
    share_near.wait_recv()

    @pl.when(core == 1)
    def _():
        make_weights(0, ROWS, 3)

    for h in range(2):
        arrived(half(images, h, ROWS), 3 + h)
        row = ROWS + h * HALF
        make_weights(row, HALF, 0)
        make_weights(row, HALF, 1)

        @pl.when(core == 0)
        def _():
            make_weights(row, HALF, 2)
            make_weights(row, HALF, 3)
            half(next_out, h)[...] = image_grad(row, HALF, 4).astype(jnp.bfloat16)

        @pl.when(core == 1)
        def _():
            half(next_out, h)[...] = image_grad(row, HALF, 2).astype(jnp.bfloat16)

        @pl.when(x < N_X - 1)
        def _():
            grad_direct[h].start()

        @pl.when(x == N_X - 1)
        def _():
            for copy in grad_spread[h]:
                copy.start()
            grad_last[h].start()

    both = pl.multiple_of((1 - core) * ROWS, ROWS)
    for t in (1, 0):
        part_out[t] = text_grad(both, ROWS, 2 + t).astype(jnp.bfloat16)
        share_part[t].start()
    grad_near = text_grad(0, 2 * ROWS, 1)
    share_part[1].wait_recv()
    text_out[...] = (grad_near + part_in[1].astype(jnp.float32)).astype(jnp.bfloat16)

    @pl.when(x == 0)
    def _():
        image_first[1].wait_send()

    @pl.when(x > 0)
    def _():
        image_relay[1].wait_send()

    @pl.when(grp_lo > 0)
    def _():
        return_text.start()

    @pl.when(x < N_X - 1)
    def _():
        for h in range(2):
            arrived(hop_grad.at[h], 9 + h)
            grad_relay[h].start()

    @pl.when(grp_lo == 0)
    def _():
        return_text.start()

    grad_t = text_grad(0, 2 * ROWS, 0)
    share_part[0].wait_recv()
    grad_t = grad_t + part_in[0].astype(jnp.float32)

    for h in range(2):
        arrived(half(next_in, h), 7 + h)

    @pl.when(core == 0)
    def _():
        gimg_ref[...] = (
            image_grad(0, ROWS, 2) + next_in[...].astype(jnp.float32)
        ).astype(jnp.bfloat16)

    @pl.when(core == 1)
    def _():
        gimg_ref[...] = (
            image_grad(0, ROWS, 4) + next_in[...].astype(jnp.float32)
        ).astype(jnp.bfloat16)

    return_text.wait_recv()
    gtxt_ref[...] = (grad_t + text_in[...].astype(jnp.float32)).astype(jnp.bfloat16)

    for copy in [send_text, share_text, share_near, return_text] + share_part:
        copy.wait_send()

    @pl.when(x == 0)
    def _():
        image_first[0].wait_send()
        for h in range(2):
            for copy in image_spread[h]:
                copy.wait_send()

    @pl.when(x > 0)
    def _():
        for h in range(2):
            image_direct[h].wait_send()
        image_relay[0].wait_send()

    @pl.when(x < N_X - 1)
    def _():
        for h in range(2):
            grad_direct[h].wait_send()
            grad_relay[h].wait_send()

    @pl.when(x == N_X - 1)
    def _():
        for h in range(2):
            grad_last[h].wait_send()
            for copy in grad_spread[h]:
                copy.wait_send()


def on_device(img, txt, sharp, shift, adj):
    shard = jax.ShapeDtypeStruct((ROWS, D), jnp.bfloat16)

    def half(rows, cols=D):
        return pltpu.VMEM((rows, cols), jnp.bfloat16)

    return pl.pallas_call(
        kernel,
        out_shape=(shard, shard),
        in_specs=[pl.BlockSpec(memory_space=pltpu.SMEM)] * 3
        + [pl.BlockSpec(memory_space=pl.ANY)] * 2,
        out_specs=[pl.BlockSpec(memory_space=pltpu.VMEM)] * 2,
        scratch_shapes=[
            half(4 * ROWS),
            half(2 * ROWS),
            half(2 * ROWS, 4 * ROWS),
            pltpu.VMEM((2, PIECE, D), jnp.bfloat16),
            pltpu.VMEM((2, PIECE, D), jnp.bfloat16),
            half(ROWS),
            half(ROWS),
            pltpu.VMEM((2, ROWS, D), jnp.bfloat16),
            pltpu.VMEM((2, ROWS, D), jnp.bfloat16),
            half(ROWS),
            half(ROWS),
            pltpu.SemaphoreType.DMA((2,)),
            pltpu.SemaphoreType.DMA((27,)),
            pltpu.SemaphoreType.DMA((14,)),
            pltpu.SemaphoreType.REGULAR,
        ],
        compiler_params=pltpu.CompilerParams(
            collective_id=0, has_side_effects=True, vmem_limit_bytes=48 << 20
        ),
        cost_estimate=pl.CostEstimate(
            flops=18 * 2 * ROWS * ROWS * D, bytes_accessed=4 * ROWS * D * 2, transcendentals=6 * ROWS * ROWS
        ),
    )(sharp, shift, adj, img, txt)


def solution(mesh):
    return jax.shard_map(
        on_device,
        mesh=mesh,
        in_specs=(P(("blk", "grp"), None), P(("blk", "grp"), None), P(), P(), P()),
        out_specs=(P(("blk", "grp"), None), P(("blk", "grp"), None)),
        check_vma=False,
    )
```

```python
import functools

import jax
import jax.numpy as jnp
from jax import lax
from jax.experimental import pallas as pl
from jax.experimental.pallas import tpu as pltpu
from jax.sharding import PartitionSpec as P

MESH = pl.DeviceIdType.MESH
ROWS = 256
D = 1152
HALF = 128
PIECE = 32
PAIRS = 196608
N_X, N_Y, N_HI, N_LO = 4, 8, 3, 4


def device(hi, x, core, y, lo):
    return ((hi * N_X + x) * 2 + core, y * N_LO + lo)


def kernel(
    sharp_ref,
    shift_ref,
    adj_ref,
    img_ref,
    txt_ref,
    gimg_ref,
    gtxt_ref,
    texts,
    images,
    weights,
    hop_img,
    hop_grad,
    next_out,
    next_in,
    part_out,
    part_in,
    text_out,
    text_in,
    load_sem,
    send_sem,
    recv_sem,
    far_sem,
    own_grad,
):
    blk = lax.axis_index("blk")
    grp = lax.axis_index("grp")
    core = lax.rem(blk, 2)
    x = lax.rem(lax.div(blk, 2), N_X)
    hi = lax.div(blk, 2 * N_X)
    grp_lo = lax.rem(grp, N_LO)
    grp_next = (blk, lax.rem(grp + 1, N_Y * N_LO))
    grp_prev = (blk, lax.rem(grp + N_Y * N_LO - 1, N_Y * N_LO))
    sibling = (blk + 1 - 2 * core, grp)
    hi_up = lax.rem(hi + 1, N_HI)
    hi_down = lax.rem(hi + N_HI - 1, N_HI)

    def line(which, at_hi):
        return ((at_hi * N_X + which) * 2 + core, grp)

    own_t, near_t, sib_t, sib_near_t = (
        texts.at[pl.ds(ROWS * n, ROWS)] for n in range(4)
    )
    own_i = images.at[pl.ds(0, ROWS)]

    load_i = pltpu.make_async_copy(img_ref, own_i, load_sem.at[0])
    load_t = pltpu.make_async_copy(txt_ref, own_t, load_sem.at[1])
    load_i.start()
    load_t.start()

    barrier = pltpu.get_barrier_semaphore()

    def greet(target):
        pl.semaphore_signal(barrier, inc=1, device_id=target, device_id_type=MESH)

    greet(grp_prev)
    greet(sibling)

    @pl.when(x == 0)
    def _():
        greet(line(1, hi))

    @pl.when(x > 0)
    def _():
        greet(line(0, hi))

    @pl.when(x == 1)
    def _():
        greet(line(2, hi))

    @pl.when(x < N_X - 1)
    def _():
        greet(line(N_X - 1, hi))

    wraps = hi == 0

    @pl.when((x == N_X - 1) & (hi < N_HI - 1))
    def _():
        for which in range(N_X):
            greet(line(which, hi_up))

    @pl.when(wraps)
    def _():
        greet(line(N_X - 1, hi_down))

    sharp = sharp_ref[0]
    shift = shift_ref[0]
    scale = adj_ref[0] * sharp / PAIRS

    def make_weights(row, rows, text, own_pair=False):
        logits = lax.dot_general(
            images[pl.ds(row, rows), :],
            texts[pl.ds(text * ROWS, ROWS), :],
            (((1,), (1,)), ((), ())),
            preferred_element_type=jnp.float32,
        )
        likely = jax.nn.sigmoid(sharp * logits + shift)
        if own_pair:
            cols = lax.broadcasted_iota(jnp.int32, likely.shape, 1)
            at_row = lax.broadcasted_iota(jnp.int32, likely.shape, 0)
            likely = likely - (cols == at_row).astype(jnp.float32)
        weights[pl.ds(row, rows), pl.ds(text * ROWS, ROWS)] = (scale * likely).astype(
            jnp.bfloat16
        )

    def image_grad(row, rows, n_texts):
        return jnp.dot(
            weights[pl.ds(row, rows), pl.ds(0, n_texts * ROWS)],
            texts[pl.ds(0, n_texts * ROWS), :],
            preferred_element_type=jnp.float32,
        )

    def text_grad(row, rows, text):
        return lax.dot_general(
            weights[pl.ds(row, rows), pl.ds(text * ROWS, ROWS)],
            images[pl.ds(row, rows), :],
            (((0,), (0,)), ((), ())),
            preferred_element_type=jnp.float32,
        )

    def send(src, dst, which, arrival, target):
        return pltpu.make_async_remote_copy(
            src_ref=src,
            dst_ref=dst,
            send_sem=send_sem.at[which],
            recv_sem=recv_sem.at[arrival],
            device_id=target,
            device_id_type=MESH,
        )

    def arrived(ref, arrival):
        send(ref, ref, 0, arrival, sibling).wait_recv()

    def half(ref, h, base=0):
        return ref.at[pl.ds(base + h * HALF, HALF)]

    def piece(ref, h, q, base=0):
        return ref.at[pl.ds(base + h * HALF + q * PIECE, PIECE)]

    up_line = line(0, hi_up)
    down_line = line(N_X - 1, hi_down)
    x_up = line(lax.rem(x + 1, N_X), hi)
    x_down = line(lax.rem(x + N_X - 1, N_X), hi)

    send_text = send(own_t, near_t, 0, 0, grp_next)
    share_text = send(own_t, sib_t, 1, 1, sibling)
    share_near = send(near_t, sib_near_t, 2, 2, sibling)
    image_direct, image_first, image_spread, image_relay = [], [], [], []
    grad_direct, grad_last, grad_spread, grad_relay = [], [], [], []
    for h in range(2):
        image_direct.append(
            send(half(images, h), half(images, h, ROWS), 3 + h, 3 + h, x_down)
        )
        image_first.append(
            send(piece(images, h, 0), piece(images, h, 0, ROWS), 3 + h, 3 + h, down_line)
        )
        image_spread.append(
            [
                send(piece(images, h, q), hop_img.at[h], 5 + 3 * h + q, 5 + h, line(q, hi))
                for q in range(1, N_X)
            ]
        )
        image_relay.append(
            send(hop_img.at[h], piece(images, h, x, ROWS), 12 + h, 3 + h, down_line)
        )
        grad_direct.append(send(half(next_out, h), half(next_in, h), 14 + h, 7 + h, x_up))
        grad_last.append(
            send(
                piece(next_out, h, N_X - 1),
                piece(next_in, h, N_X - 1),
                14 + h,
                7 + h,
                up_line,
            )
        )
        grad_spread.append(
            [
                send(piece(next_out, h, q), hop_grad.at[h], 16 + 3 * h + q, 9 + h, line(q, hi))
                for q in range(N_X - 1)
            ]
        )
        grad_relay.append(
            send(hop_grad.at[h], piece(next_in, h, x), 22 + h, 7 + h, up_line)
        )
    share_part = [send(part_out.at[t], part_in.at[t], 24 + t, 11 + t, sibling) for t in range(2)]
    return_text = send(text_out, text_in, 26, 13, grp_prev)

    load_i.wait()
    load_t.wait()
    make_weights(0, ROWS, 0, own_pair=True)
    first = jnp.where((x == 0) | (x == N_X - 1), 5, 3)
    first = first + jnp.where(hi > 0, 1, 0)
    first = first + jnp.where((x == N_X - 1) & (hi == N_HI - 1), N_X, 0)
    pl.semaphore_wait(barrier, first)

    @pl.when((x == N_X - 1) & (hi == N_HI - 1))
    def _():
        for which in range(N_X):
            pl.semaphore_signal(
                far_sem, inc=1, device_id=line(which, hi_up), device_id_type=MESH
            )

    def await_far():
        @pl.when(wraps)
        def _():
            pl.semaphore_wait(far_sem, 1)

    @pl.when(x == 0)
    def _():
        for h in range(2):
            for copy in image_spread[h]:
                copy.start()

    @pl.when(x > 0)
    def _():
        for h in range(2):
            image_direct[h].start()

    send_text.start()
    share_text.start()

    await_far()

    @pl.when(x == 0)
    def _():
        for h in (0,):
            image_first[h].start()

    @pl.when(x > 0)
    def _():
        for h in (0,):
            arrived(hop_img.at[h], 5 + h)
            image_relay[h].start()

    share_text.wait_recv()

    @pl.when(core == 1)
    def _():
        make_weights(0, ROWS, 2)

    @pl.when(x < N_X - 1)
    def _():
        for h in range(2):
            arrived(half(images, h, ROWS), 3 + h)
        make_weights(ROWS, ROWS, 0)

        @pl.when(core == 0)
        def _():
            make_weights(ROWS, ROWS, 2)

    send_text.wait_recv()
    share_near.start()
    @pl.when(x == 0)
    def _():
        for h in (1,):
            image_first[h].start()

    @pl.when(x > 0)
    def _():
        for h in (1,):
            arrived(hop_img.at[h], 5 + h)
            image_relay[h].start()


    make_weights(0, ROWS, 1)
    share_near.wait_recv()

    @pl.when(core == 1)
    def _():
        make_weights(0, ROWS, 3)

    for h in range(2):
        row = ROWS + h * HALF

        @pl.when(x == N_X - 1)
        def _():
            arrived(half(images, h, ROWS), 3 + h)
            make_weights(row, HALF, 0)

            @pl.when(core == 0)
            def _():
                make_weights(row, HALF, 2)

        make_weights(row, HALF, 1)

        @pl.when(core == 0)
        def _():
            make_weights(row, HALF, 3)
            half(next_out, h)[...] = image_grad(row, HALF, 4).astype(jnp.bfloat16)

        @pl.when(core == 1)
        def _():
            half(next_out, h)[...] = image_grad(row, HALF, 2).astype(jnp.bfloat16)

        @pl.when(x < N_X - 1)
        def _():
            grad_direct[h].start()

        @pl.when(x == N_X - 1)
        def _():
            for copy in grad_spread[h]:
                copy.start()
            grad_last[h].start()

    both = pl.multiple_of((1 - core) * ROWS, ROWS)
    for t in (1, 0):
        part_out[t] = text_grad(both, ROWS, 2 + t).astype(jnp.bfloat16)
        share_part[t].start()
    grad_near = text_grad(0, 2 * ROWS, 1)
    share_part[1].wait_recv()
    text_out[...] = (grad_near + part_in[1].astype(jnp.float32)).astype(jnp.bfloat16)

    @pl.when(x == 0)
    def _():
        image_first[1].wait_send()

    @pl.when(x > 0)
    def _():
        image_relay[1].wait_send()

    @pl.when(grp_lo > 0)
    def _():
        return_text.start()

    @pl.when(x < N_X - 1)
    def _():
        for h in range(2):
            arrived(hop_grad.at[h], 9 + h)
            grad_relay[h].start()

    @pl.when(grp_lo == 0)
    def _():
        return_text.start()

    grad_t = text_grad(0, 2 * ROWS, 0)
    share_part[0].wait_recv()
    grad_t = grad_t + part_in[0].astype(jnp.float32)

    @pl.when(core == 0)
    def _():
        own_grad[...] = image_grad(0, ROWS, 2)

    @pl.when(core == 1)
    def _():
        own_grad[...] = image_grad(0, ROWS, 4)

    for h in range(2):
        arrived(half(next_in, h), 7 + h)
    gimg_ref[...] = (own_grad[...] + next_in[...].astype(jnp.float32)).astype(jnp.bfloat16)

    return_text.wait_recv()
    gtxt_ref[...] = (grad_t + text_in[...].astype(jnp.float32)).astype(jnp.bfloat16)

    for copy in [send_text, share_text, share_near, return_text] + share_part:
        copy.wait_send()

    @pl.when(x == 0)
    def _():
        image_first[0].wait_send()
        for h in range(2):
            for copy in image_spread[h]:
                copy.wait_send()

    @pl.when(x > 0)
    def _():
        for h in range(2):
            image_direct[h].wait_send()
        image_relay[0].wait_send()

    @pl.when(x < N_X - 1)
    def _():
        for h in range(2):
            grad_direct[h].wait_send()
            grad_relay[h].wait_send()

    @pl.when(x == N_X - 1)
    def _():
        for h in range(2):
            grad_last[h].wait_send()
            for copy in grad_spread[h]:
                copy.wait_send()


def on_device(img, txt, sharp, shift, adj):
    shard = jax.ShapeDtypeStruct((ROWS, D), jnp.bfloat16)

    def half(rows, cols=D):
        return pltpu.VMEM((rows, cols), jnp.bfloat16)

    return pl.pallas_call(
        kernel,
        out_shape=(shard, shard),
        in_specs=[pl.BlockSpec(memory_space=pltpu.SMEM)] * 3
        + [pl.BlockSpec(memory_space=pl.ANY)] * 2,
        out_specs=[pl.BlockSpec(memory_space=pltpu.VMEM)] * 2,
        scratch_shapes=[
            half(4 * ROWS),
            half(2 * ROWS),
            half(2 * ROWS, 4 * ROWS),
            pltpu.VMEM((2, PIECE, D), jnp.bfloat16),
            pltpu.VMEM((2, PIECE, D), jnp.bfloat16),
            half(ROWS),
            half(ROWS),
            pltpu.VMEM((2, ROWS, D), jnp.bfloat16),
            pltpu.VMEM((2, ROWS, D), jnp.bfloat16),
            half(ROWS),
            half(ROWS),
            pltpu.SemaphoreType.DMA((2,)),
            pltpu.SemaphoreType.DMA((27,)),
            pltpu.SemaphoreType.DMA((14,)),
            pltpu.SemaphoreType.REGULAR,
            pltpu.VMEM((ROWS, D), jnp.float32),
        ],
        compiler_params=pltpu.CompilerParams(
            collective_id=0, has_side_effects=True, vmem_limit_bytes=60 << 20
        ),
        cost_estimate=pl.CostEstimate(
            flops=18 * 2 * ROWS * ROWS * D, bytes_accessed=4 * ROWS * D * 2, transcendentals=6 * ROWS * ROWS
        ),
    )(sharp, shift, adj, img, txt)


def solution(mesh):
    return jax.shard_map(
        on_device,
        mesh=mesh,
        in_specs=(P(("blk", "grp"), None), P(("blk", "grp"), None), P(), P(), P()),
        out_specs=(P(("blk", "grp"), None), P(("blk", "grp"), None)),
        check_vma=False,
    )
```

```python
import functools

import jax
import jax.numpy as jnp
from jax import lax
from jax.experimental import pallas as pl
from jax.experimental.pallas import tpu as pltpu
from jax.sharding import PartitionSpec as P

MESH = pl.DeviceIdType.MESH
ROWS = 256
D = 1152
HALF = 128
PIECE = 32
PAIRS = 196608
N_X, N_Y, N_HI, N_LO = 4, 8, 3, 4


def device(hi, x, core, y, lo):
    return ((hi * N_X + x) * 2 + core, y * N_LO + lo)


def kernel(
    sharp_ref,
    shift_ref,
    adj_ref,
    img_ref,
    txt_ref,
    gimg_ref,
    gtxt_ref,
    texts,
    images,
    weights,
    hop_img,
    hop_grad,
    next_out,
    next_in,
    part_out,
    part_in,
    text_out,
    text_in,
    load_sem,
    send_sem,
    recv_sem,
    far_sem,
    own_grad,
):
    blk = lax.axis_index("blk")
    grp = lax.axis_index("grp")
    core = lax.rem(blk, 2)
    x = lax.rem(lax.div(blk, 2), N_X)
    hi = lax.div(blk, 2 * N_X)
    grp_lo = lax.rem(grp, N_LO)
    grp_next = (blk, lax.rem(grp + 1, N_Y * N_LO))
    grp_prev = (blk, lax.rem(grp + N_Y * N_LO - 1, N_Y * N_LO))
    sibling = (blk + 1 - 2 * core, grp)
    hi_up = lax.rem(hi + 1, N_HI)
    hi_down = lax.rem(hi + N_HI - 1, N_HI)

    def line(which, at_hi):
        return ((at_hi * N_X + which) * 2 + core, grp)

    own_t, near_t, sib_t, sib_near_t = (
        texts.at[pl.ds(ROWS * n, ROWS)] for n in range(4)
    )
    own_i = images.at[pl.ds(0, ROWS)]

    load_i = pltpu.make_async_copy(img_ref, own_i, load_sem.at[0])
    load_t = pltpu.make_async_copy(txt_ref, own_t, load_sem.at[1])
    load_i.start()
    load_t.start()

    barrier = pltpu.get_barrier_semaphore()

    def greet(target):
        pl.semaphore_signal(barrier, inc=1, device_id=target, device_id_type=MESH)

    greet(grp_prev)
    greet(sibling)

    @pl.when(x == 0)
    def _():
        greet(line(1, hi))

    @pl.when(x > 0)
    def _():
        greet(line(0, hi))

    @pl.when(x == 1)
    def _():
        greet(line(2, hi))

    @pl.when(x < N_X - 1)
    def _():
        greet(line(N_X - 1, hi))

    wraps = hi == 0

    @pl.when((x == N_X - 1) & (hi < N_HI - 1))
    def _():
        for which in range(N_X):
            greet(line(which, hi_up))

    @pl.when(wraps)
    def _():
        greet(line(N_X - 1, hi_down))

    sharp = sharp_ref[0]
    shift = shift_ref[0]
    scale = adj_ref[0] * sharp / PAIRS

    def make_weights(row, rows, text, own_pair=False):
        logits = lax.dot_general(
            images[pl.ds(row, rows), :],
            texts[pl.ds(text * ROWS, ROWS), :],
            (((1,), (1,)), ((), ())),
            preferred_element_type=jnp.float32,
        )
        likely = jax.nn.sigmoid(sharp * logits + shift)
        if own_pair:
            cols = lax.broadcasted_iota(jnp.int32, likely.shape, 1)
            at_row = lax.broadcasted_iota(jnp.int32, likely.shape, 0)
            likely = likely - (cols == at_row).astype(jnp.float32)
        weights[pl.ds(row, rows), pl.ds(text * ROWS, ROWS)] = (scale * likely).astype(
            jnp.bfloat16
        )

    def image_grad(row, rows, n_texts):
        return jnp.dot(
            weights[pl.ds(row, rows), pl.ds(0, n_texts * ROWS)],
            texts[pl.ds(0, n_texts * ROWS), :],
            preferred_element_type=jnp.float32,
        )

    def text_grad(row, rows, text):
        return lax.dot_general(
            weights[pl.ds(row, rows), pl.ds(text * ROWS, ROWS)],
            images[pl.ds(row, rows), :],
            (((0,), (0,)), ((), ())),
            preferred_element_type=jnp.float32,
        )

    def send(src, dst, which, arrival, target):
        return pltpu.make_async_remote_copy(
            src_ref=src,
            dst_ref=dst,
            send_sem=send_sem.at[which],
            recv_sem=recv_sem.at[arrival],
            device_id=target,
            device_id_type=MESH,
        )

    def arrived(ref, arrival):
        send(ref, ref, 0, arrival, sibling).wait_recv()

    def half(ref, h, base=0):
        return ref.at[pl.ds(base + h * HALF, HALF)]

    def piece(ref, h, q, base=0):
        return ref.at[pl.ds(base + h * HALF + q * PIECE, PIECE)]

    up_line = line(0, hi_up)
    down_line = line(N_X - 1, hi_down)
    x_up = line(lax.rem(x + 1, N_X), hi)
    x_down = line(lax.rem(x + N_X - 1, N_X), hi)

    send_text = send(own_t, near_t, 0, 0, grp_next)
    share_text = send(own_t, sib_t, 1, 1, sibling)
    share_near = send(near_t, sib_near_t, 2, 2, sibling)
    image_direct, image_first, image_spread, image_relay = [], [], [], []
    grad_direct, grad_last, grad_spread, grad_relay = [], [], [], []
    for h in range(2):
        image_direct.append(
            send(half(images, h), half(images, h, ROWS), 3 + h, 3 + h, x_down)
        )
        image_first.append(
            send(piece(images, h, 0), piece(images, h, 0, ROWS), 3 + h, 3 + h, down_line)
        )
        image_spread.append(
            [
                send(piece(images, h, q), hop_img.at[h], 5 + 3 * h + q, 5 + h, line(q, hi))
                for q in range(1, N_X)
            ]
        )
        image_relay.append(
            send(hop_img.at[h], piece(images, h, x, ROWS), 12 + h, 3 + h, down_line)
        )
        grad_direct.append(send(half(next_out, h), half(next_in, h), 14 + h, 7 + h, x_up))
        grad_last.append(
            send(
                piece(next_out, h, N_X - 1),
                piece(next_in, h, N_X - 1),
                14 + h,
                7 + h,
                up_line,
            )
        )
        grad_spread.append(
            [
                send(piece(next_out, h, q), hop_grad.at[h], 16 + 3 * h + q, 9 + h, line(q, hi))
                for q in range(N_X - 1)
            ]
        )
        grad_relay.append(
            send(hop_grad.at[h], piece(next_in, h, x), 22 + h, 7 + h, up_line)
        )
    share_part = [send(part_out.at[t], part_in.at[t], 24 + t, 11 + t, sibling) for t in range(2)]
    return_text = send(text_out, text_in, 26, 13, grp_prev)

    load_i.wait()
    load_t.wait()
    make_weights(0, ROWS, 0, own_pair=True)
    first = jnp.where((x == 0) | (x == N_X - 1), 5, 3)
    first = first + jnp.where(hi > 0, 1, 0)
    first = first + jnp.where((x == N_X - 1) & (hi == N_HI - 1), N_X, 0)
    pl.semaphore_wait(barrier, first)

    @pl.when((x == N_X - 1) & (hi == N_HI - 1))
    def _():
        for which in range(N_X):
            pl.semaphore_signal(
                far_sem, inc=1, device_id=line(which, hi_up), device_id_type=MESH
            )

    def await_far():
        @pl.when(wraps)
        def _():
            pl.semaphore_wait(far_sem, 1)

    @pl.when(x == 0)
    def _():
        for h in range(2):
            for copy in image_spread[h]:
                copy.start()

    @pl.when(x > 0)
    def _():
        for h in range(2):
            image_direct[h].start()

    send_text.start()
    share_text.start()

    await_far()

    @pl.when(x == 0)
    def _():
        for h in (0,):
            image_first[h].start()

    @pl.when(x > 0)
    def _():
        for h in (0,):
            arrived(hop_img.at[h], 5 + h)
            image_relay[h].start()

    share_text.wait_recv()

    @pl.when(core == 1)
    def _():
        make_weights(0, ROWS, 2)

    send_text.wait_recv()
    share_near.start()
    @pl.when(x == 0)
    def _():
        for h in (1,):
            image_first[h].start()

    @pl.when(x > 0)
    def _():
        for h in (1,):
            arrived(hop_img.at[h], 5 + h)
            image_relay[h].start()


    make_weights(0, ROWS, 1)
    share_near.wait_recv()

    @pl.when(core == 1)
    def _():
        make_weights(0, ROWS, 3)

    for h in range(2):
        arrived(half(images, h, ROWS), 3 + h)
        row = ROWS + h * HALF
        make_weights(row, HALF, 0)
        make_weights(row, HALF, 1)

        @pl.when(core == 0)
        def _():
            make_weights(row, HALF, 2)
            make_weights(row, HALF, 3)
            half(next_out, h)[...] = image_grad(row, HALF, 4).astype(jnp.bfloat16)

        @pl.when(core == 1)
        def _():
            half(next_out, h)[...] = image_grad(row, HALF, 2).astype(jnp.bfloat16)

        @pl.when(x < N_X - 1)
        def _():
            grad_direct[h].start()

        @pl.when(x == N_X - 1)
        def _():
            for copy in grad_spread[h]:
                copy.start()
            grad_last[h].start()

    both = pl.multiple_of((1 - core) * ROWS, ROWS)
    part_out[1] = text_grad(both, ROWS, 3).astype(jnp.bfloat16)
    share_part[1].start()
    grad_near = text_grad(0, 2 * ROWS, 1)
    share_part[1].wait_recv()
    text_out[...] = (grad_near + part_in[1].astype(jnp.float32)).astype(jnp.bfloat16)

    @pl.when(x == 0)
    def _():
        image_first[1].wait_send()

    @pl.when(x > 0)
    def _():
        image_relay[1].wait_send()

    @pl.when(grp_lo > 0)
    def _():
        return_text.start()

    @pl.when(x < N_X - 1)
    def _():
        for h in range(2):
            arrived(hop_grad.at[h], 9 + h)
            grad_relay[h].start()

    @pl.when(grp_lo == 0)
    def _():
        return_text.start()

    part_out[0] = text_grad(both, ROWS, 2).astype(jnp.bfloat16)
    share_part[0].start()
    grad_t = text_grad(0, 2 * ROWS, 0)
    share_part[0].wait_recv()
    grad_t = grad_t + part_in[0].astype(jnp.float32)

    @pl.when(core == 0)
    def _():
        own_grad[...] = image_grad(0, ROWS, 2)

    @pl.when(core == 1)
    def _():
        own_grad[...] = image_grad(0, ROWS, 4)

    for h in range(2):
        arrived(half(next_in, h), 7 + h)
    gimg_ref[...] = (own_grad[...] + next_in[...].astype(jnp.float32)).astype(jnp.bfloat16)

    return_text.wait_recv()
    gtxt_ref[...] = (grad_t + text_in[...].astype(jnp.float32)).astype(jnp.bfloat16)

    for copy in [send_text, share_text, share_near, return_text] + share_part:
        copy.wait_send()

    @pl.when(x == 0)
    def _():
        image_first[0].wait_send()
        for h in range(2):
            for copy in image_spread[h]:
                copy.wait_send()

    @pl.when(x > 0)
    def _():
        for h in range(2):
            image_direct[h].wait_send()
        image_relay[0].wait_send()

    @pl.when(x < N_X - 1)
    def _():
        for h in range(2):
            grad_direct[h].wait_send()
            grad_relay[h].wait_send()

    @pl.when(x == N_X - 1)
    def _():
        for h in range(2):
            grad_last[h].wait_send()
            for copy in grad_spread[h]:
                copy.wait_send()


def on_device(img, txt, sharp, shift, adj):
    shard = jax.ShapeDtypeStruct((ROWS, D), jnp.bfloat16)

    def half(rows, cols=D):
        return pltpu.VMEM((rows, cols), jnp.bfloat16)

    return pl.pallas_call(
        kernel,
        out_shape=(shard, shard),
        in_specs=[pl.BlockSpec(memory_space=pltpu.SMEM)] * 3
        + [pl.BlockSpec(memory_space=pl.ANY)] * 2,
        out_specs=[pl.BlockSpec(memory_space=pltpu.VMEM)] * 2,
        scratch_shapes=[
            half(4 * ROWS),
            half(2 * ROWS),
            half(2 * ROWS, 4 * ROWS),
            pltpu.VMEM((2, PIECE, D), jnp.bfloat16),
            pltpu.VMEM((2, PIECE, D), jnp.bfloat16),
            half(ROWS),
            half(ROWS),
            pltpu.VMEM((2, ROWS, D), jnp.bfloat16),
            pltpu.VMEM((2, ROWS, D), jnp.bfloat16),
            half(ROWS),
            half(ROWS),
            pltpu.SemaphoreType.DMA((2,)),
            pltpu.SemaphoreType.DMA((27,)),
            pltpu.SemaphoreType.DMA((14,)),
            pltpu.SemaphoreType.REGULAR,
            pltpu.VMEM((ROWS, D), jnp.float32),
        ],
        compiler_params=pltpu.CompilerParams(
            collective_id=0, has_side_effects=True, vmem_limit_bytes=48 << 20
        ),
        cost_estimate=pl.CostEstimate(
            flops=18 * 2 * ROWS * ROWS * D, bytes_accessed=4 * ROWS * D * 2, transcendentals=6 * ROWS * ROWS
        ),
    )(sharp, shift, adj, img, txt)


def solution(mesh):
    return jax.shard_map(
        on_device,
        mesh=mesh,
        in_specs=(P(("blk", "grp"), None), P(("blk", "grp"), None), P(), P(), P()),
        out_specs=(P(("blk", "grp"), None), P(("blk", "grp"), None)),
        check_vma=False,
    )
```

```python
import functools

import jax
import jax.numpy as jnp
from jax import lax
from jax.experimental import pallas as pl
from jax.experimental.pallas import tpu as pltpu
from jax.sharding import PartitionSpec as P

MESH = pl.DeviceIdType.MESH
ROWS = 256
D = 1152
HALF = 128
PIECE = 32
PAIRS = 196608
N_X, N_Y, N_HI, N_LO = 4, 8, 3, 4


def device(hi, x, core, y, lo):
    return ((hi * N_X + x) * 2 + core, y * N_LO + lo)


def kernel(
    sharp_ref,
    shift_ref,
    adj_ref,
    img_ref,
    txt_ref,
    gimg_ref,
    gtxt_ref,
    texts,
    images,
    weights,
    hop_img,
    hop_grad,
    next_out,
    next_in,
    part_out,
    part_in,
    text_out,
    text_in,
    load_sem,
    send_sem,
    recv_sem,
    far_sem,
    own_grad,
):
    blk = lax.axis_index("blk")
    grp = lax.axis_index("grp")
    core = lax.rem(blk, 2)
    x = lax.rem(lax.div(blk, 2), N_X)
    hi = lax.div(blk, 2 * N_X)
    grp_lo = lax.rem(grp, N_LO)
    grp_next = (blk, lax.rem(grp + 1, N_Y * N_LO))
    grp_prev = (blk, lax.rem(grp + N_Y * N_LO - 1, N_Y * N_LO))
    sibling = (blk + 1 - 2 * core, grp)
    hi_up = lax.rem(hi + 1, N_HI)
    hi_down = lax.rem(hi + N_HI - 1, N_HI)

    def line(which, at_hi):
        return ((at_hi * N_X + which) * 2 + core, grp)

    own_t, near_t, sib_t, sib_near_t = (
        texts.at[pl.ds(ROWS * n, ROWS)] for n in range(4)
    )
    own_i = images.at[pl.ds(0, ROWS)]

    load_i = pltpu.make_async_copy(img_ref, own_i, load_sem.at[0])
    load_t = pltpu.make_async_copy(txt_ref, own_t, load_sem.at[1])
    load_i.start()
    load_t.start()

    barrier = pltpu.get_barrier_semaphore()

    def greet(target):
        pl.semaphore_signal(barrier, inc=1, device_id=target, device_id_type=MESH)

    greet(grp_prev)
    greet(sibling)

    @pl.when(x == 0)
    def _():
        greet(line(1, hi))

    @pl.when(x > 0)
    def _():
        greet(line(0, hi))

    @pl.when(x == 1)
    def _():
        greet(line(2, hi))

    @pl.when(x < N_X - 1)
    def _():
        greet(line(N_X - 1, hi))

    wraps = hi == 0

    @pl.when((x == N_X - 1) & (hi < N_HI - 1))
    def _():
        for which in range(N_X):
            greet(line(which, hi_up))

    @pl.when(wraps)
    def _():
        greet(line(N_X - 1, hi_down))

    sharp = sharp_ref[0]
    shift = shift_ref[0]
    scale = adj_ref[0] * sharp / PAIRS

    def make_weights(row, rows, text, own_pair=False):
        logits = lax.dot_general(
            images[pl.ds(row, rows), :],
            texts[pl.ds(text * ROWS, ROWS), :],
            (((1,), (1,)), ((), ())),
            preferred_element_type=jnp.float32,
        )
        likely = jax.nn.sigmoid(sharp * logits + shift)
        if own_pair:
            cols = lax.broadcasted_iota(jnp.int32, likely.shape, 1)
            at_row = lax.broadcasted_iota(jnp.int32, likely.shape, 0)
            likely = likely - (cols == at_row).astype(jnp.float32)
        weights[pl.ds(row, rows), pl.ds(text * ROWS, ROWS)] = (scale * likely).astype(
            jnp.bfloat16
        )

    def image_grad(row, rows, n_texts):
        return jnp.dot(
            weights[pl.ds(row, rows), pl.ds(0, n_texts * ROWS)],
            texts[pl.ds(0, n_texts * ROWS), :],
            preferred_element_type=jnp.float32,
        )

    def text_grad(row, rows, text):
        return lax.dot_general(
            weights[pl.ds(row, rows), pl.ds(text * ROWS, ROWS)],
            images[pl.ds(row, rows), :],
            (((0,), (0,)), ((), ())),
            preferred_element_type=jnp.float32,
        )

    def send(src, dst, which, arrival, target):
        return pltpu.make_async_remote_copy(
            src_ref=src,
            dst_ref=dst,
            send_sem=send_sem.at[which],
            recv_sem=recv_sem.at[arrival],
            device_id=target,
            device_id_type=MESH,
        )

    def arrived(ref, arrival):
        send(ref, ref, 0, arrival, sibling).wait_recv()

    def half(ref, h, base=0):
        return ref.at[pl.ds(base + h * HALF, HALF)]

    def piece(ref, h, q, base=0):
        return ref.at[pl.ds(base + h * HALF + q * PIECE, PIECE)]

    up_line = line(0, hi_up)
    down_line = line(N_X - 1, hi_down)
    x_up = line(lax.rem(x + 1, N_X), hi)
    x_down = line(lax.rem(x + N_X - 1, N_X), hi)

    send_text = send(own_t, near_t, 0, 0, grp_next)
    share_text = send(own_t, sib_t, 1, 1, sibling)
    share_near = send(near_t, sib_near_t, 2, 2, sibling)
    image_direct, image_first, image_spread, image_relay = [], [], [], []
    grad_direct, grad_last, grad_spread, grad_relay = [], [], [], []
    for h in range(2):
        image_direct.append(
            send(half(images, h), half(images, h, ROWS), 3 + h, 3 + h, x_down)
        )
        image_first.append(
            send(piece(images, h, 0), piece(images, h, 0, ROWS), 3 + h, 3 + h, down_line)
        )
        image_spread.append(
            [
                send(piece(images, h, q), hop_img.at[h], 5 + 3 * h + q, 5 + h, line(q, hi))
                for q in range(1, N_X)
            ]
        )
        image_relay.append(
            send(hop_img.at[h], piece(images, h, x, ROWS), 12 + h, 3 + h, down_line)
        )
        grad_direct.append(send(half(next_out, h), half(next_in, h), 14 + h, 7 + h, x_up))
        grad_last.append(
            send(
                piece(next_out, h, N_X - 1),
                piece(next_in, h, N_X - 1),
                14 + h,
                7 + h,
                up_line,
            )
        )
        grad_spread.append(
            [
                send(piece(next_out, h, q), hop_grad.at[h], 16 + 3 * h + q, 9 + h, line(q, hi))
                for q in range(N_X - 1)
            ]
        )
        grad_relay.append(
            send(hop_grad.at[h], piece(next_in, h, x), 22 + h, 7 + h, up_line)
        )
    share_part = [send(part_out.at[t], part_in.at[t], 24 + t, 11 + t, sibling) for t in range(2)]
    return_text = send(text_out, text_in, 26, 13, grp_prev)

    load_i.wait()
    load_t.wait()
    make_weights(0, ROWS, 0, own_pair=True)
    first = jnp.where((x == 0) | (x == N_X - 1), 5, 3)
    first = first + jnp.where(hi > 0, 1, 0)
    first = first + jnp.where((x == N_X - 1) & (hi == N_HI - 1), N_X, 0)
    pl.semaphore_wait(barrier, first)

    @pl.when((x == N_X - 1) & (hi == N_HI - 1))
    def _():
        for which in range(N_X):
            pl.semaphore_signal(
                far_sem, inc=1, device_id=line(which, hi_up), device_id_type=MESH
            )

    def await_far():
        @pl.when(wraps)
        def _():
            pl.semaphore_wait(far_sem, 1)

    @pl.when(x == 0)
    def _():
        for h in range(2):
            for copy in image_spread[h]:
                copy.start()

    @pl.when(x > 0)
    def _():
        for h in range(2):
            image_direct[h].start()

    send_text.start()
    share_text.start()

    await_far()
    hold = (hi > 0, hi >= 0)

    @pl.when((x == 0) & (jnp.logical_not(hold[0])))
    def _():
        image_first[0].start()

    @pl.when((x > 0) & (jnp.logical_not(hold[0])))
    def _():
        arrived(hop_img.at[0], 5)
        image_relay[0].start()

    @pl.when((x == 0) & (jnp.logical_not(hold[1])))
    def _():
        image_first[1].start()

    @pl.when((x > 0) & (jnp.logical_not(hold[1])))
    def _():
        arrived(hop_img.at[1], 6)
        image_relay[1].start()

    share_text.wait_recv()

    @pl.when(core == 1)
    def _():
        make_weights(0, ROWS, 2)

    send_text.wait_recv()
    share_near.start()

    @pl.when((x == 0) & (hold[0]))
    def _():
        image_first[0].start()

    @pl.when((x > 0) & (hold[0]))
    def _():
        arrived(hop_img.at[0], 5)
        image_relay[0].start()

    @pl.when((x == 0) & (hold[1]))
    def _():
        image_first[1].start()

    @pl.when((x > 0) & (hold[1]))
    def _():
        arrived(hop_img.at[1], 6)
        image_relay[1].start()

    make_weights(0, ROWS, 1)
    share_near.wait_recv()

    @pl.when(core == 1)
    def _():
        make_weights(0, ROWS, 3)

    for h in range(2):
        arrived(half(images, h, ROWS), 3 + h)
        row = ROWS + h * HALF
        make_weights(row, HALF, 0)
        make_weights(row, HALF, 1)

        @pl.when(core == 0)
        def _():
            make_weights(row, HALF, 2)
            make_weights(row, HALF, 3)
            half(next_out, h)[...] = image_grad(row, HALF, 4).astype(jnp.bfloat16)

        @pl.when(core == 1)
        def _():
            half(next_out, h)[...] = image_grad(row, HALF, 2).astype(jnp.bfloat16)

        @pl.when(x < N_X - 1)
        def _():
            grad_direct[h].start()

        @pl.when(x == N_X - 1)
        def _():
            for copy in grad_spread[h]:
                copy.start()
            grad_last[h].start()

    both = pl.multiple_of((1 - core) * ROWS, ROWS)
    part_out[1] = text_grad(both, ROWS, 3).astype(jnp.bfloat16)
    share_part[1].start()
    grad_near = text_grad(0, 2 * ROWS, 1)
    share_part[1].wait_recv()
    text_out[...] = (grad_near + part_in[1].astype(jnp.float32)).astype(jnp.bfloat16)

    @pl.when(x == 0)
    def _():
        image_first[1].wait_send()

    @pl.when(x > 0)
    def _():
        image_relay[1].wait_send()

    late = (grp_lo == 0) & (hi == N_HI - 1)

    @pl.when(jnp.logical_not(late))
    def _():
        return_text.start()

    @pl.when(x < N_X - 1)
    def _():
        for h in range(2):
            arrived(hop_grad.at[h], 9 + h)
            grad_relay[h].start()

    @pl.when(late)
    def _():
        return_text.start()

    part_out[0] = text_grad(both, ROWS, 2).astype(jnp.bfloat16)
    share_part[0].start()
    grad_t = text_grad(0, 2 * ROWS, 0)
    share_part[0].wait_recv()
    grad_t = grad_t + part_in[0].astype(jnp.float32)

    @pl.when(core == 0)
    def _():
        own_grad[...] = image_grad(0, ROWS, 2)

    @pl.when(core == 1)
    def _():
        own_grad[...] = image_grad(0, ROWS, 4)

    for h in range(2):
        arrived(half(next_in, h), 7 + h)
    gimg_ref[...] = (own_grad[...] + next_in[...].astype(jnp.float32)).astype(jnp.bfloat16)

    return_text.wait_recv()
    gtxt_ref[...] = (grad_t + text_in[...].astype(jnp.float32)).astype(jnp.bfloat16)

    for copy in [send_text, share_text, share_near, return_text] + share_part:
        copy.wait_send()

    @pl.when(x == 0)
    def _():
        image_first[0].wait_send()
        for h in range(2):
            for copy in image_spread[h]:
                copy.wait_send()

    @pl.when(x > 0)
    def _():
        for h in range(2):
            image_direct[h].wait_send()
        image_relay[0].wait_send()

    @pl.when(x < N_X - 1)
    def _():
        for h in range(2):
            grad_direct[h].wait_send()
            grad_relay[h].wait_send()

    @pl.when(x == N_X - 1)
    def _():
        for h in range(2):
            grad_last[h].wait_send()
            for copy in grad_spread[h]:
                copy.wait_send()


def on_device(img, txt, sharp, shift, adj):
    shard = jax.ShapeDtypeStruct((ROWS, D), jnp.bfloat16)

    def half(rows, cols=D):
        return pltpu.VMEM((rows, cols), jnp.bfloat16)

    return pl.pallas_call(
        kernel,
        out_shape=(shard, shard),
        in_specs=[pl.BlockSpec(memory_space=pltpu.SMEM)] * 3
        + [pl.BlockSpec(memory_space=pl.ANY)] * 2,
        out_specs=[pl.BlockSpec(memory_space=pltpu.VMEM)] * 2,
        scratch_shapes=[
            half(4 * ROWS),
            half(2 * ROWS),
            half(2 * ROWS, 4 * ROWS),
            pltpu.VMEM((2, PIECE, D), jnp.bfloat16),
            pltpu.VMEM((2, PIECE, D), jnp.bfloat16),
            half(ROWS),
            half(ROWS),
            pltpu.VMEM((2, ROWS, D), jnp.bfloat16),
            pltpu.VMEM((2, ROWS, D), jnp.bfloat16),
            half(ROWS),
            half(ROWS),
            pltpu.SemaphoreType.DMA((2,)),
            pltpu.SemaphoreType.DMA((27,)),
            pltpu.SemaphoreType.DMA((14,)),
            pltpu.SemaphoreType.REGULAR,
            pltpu.VMEM((ROWS, D), jnp.float32),
        ],
        compiler_params=pltpu.CompilerParams(
            collective_id=0, has_side_effects=True, vmem_limit_bytes=60 << 20
        ),
        cost_estimate=pl.CostEstimate(
            flops=18 * 2 * ROWS * ROWS * D, bytes_accessed=4 * ROWS * D * 2, transcendentals=6 * ROWS * ROWS
        ),
    )(sharp, shift, adj, img, txt)


def solution(mesh):
    return jax.shard_map(
        on_device,
        mesh=mesh,
        in_specs=(P(("blk", "grp"), None), P(("blk", "grp"), None), P(), P(), P()),
        out_specs=(P(("blk", "grp"), None), P(("blk", "grp"), None)),
        check_vma=False,
    )
```
